512 devices in a mesh: blk: 128 (over y, z, core), ex: 4 (over x).
Axes of the slice: x: 4, y: 4, z: 16, core: 2. Of those that a mesh axis runs over, the one named last changes fastest.
Arguments:
- hidden: bfloat16 [16, 256, 11008], P('ex', None, 'blk'), may hold values from -6 to 6
- out_grad: bfloat16 [16, 256, 4096], P('ex', None, 'blk'), may hold values from -0.5625 to 0.5625
- example_len: int32 [16], P('ex'), may hold values from 1 to 256, 2048 in all
- sign_bits: int32 [16384, 4096], P('blk'), may hold values 0 or 1
- kept_rows: int32 [8192], replicated, may hold values from 0 to 16383
- kept_cols: int32 [8192], replicated, may hold values from 0 to 4095
Outputs:
- sketch: float32 [16, 8192], P(None, ('blk', 'ex'))
The draws below stay inside these ranges and needn't reach their ends.
All inputs are finite; a program needn't handle non-finite values. No bound on the sum of `example_len` or of `sign_bits` on one device may be relied on, other than what follows from the above.
Results may differ from the reference program's by a relative error of at most 0.0003.
Values may be sent and summed in bfloat16 or wider, within the bound.
A program may use at most 64 MiB of HBM per device.

```python
import math
import jax
import jax.numpy as jnp
import numpy as np
from jax import lax

D = 4096
FF = 11008
HL = 67108864
KEEP = 8192
SEQ = 256
EXAMPLES = 16
ROWS_P = 16384
N_BLK = 128


def plant(entries, key, least, high):
    longest = entries.shape.index(max(entries.shape))
    spots = []
    for shift in (0, 1):
        where = [jax.random.randint(jax.random.fold_in(key, axis), (), 0, length) for axis, length in enumerate(entries.shape)]
        where[longest] = (where[longest] + shift) % entries.shape[longest]
        spots.append(tuple(where))
    return entries.at[spots[0]].set(least).at[spots[1]].set(high)


def shard_levels(key, dims, cuts, low, largest):
    loudness, own = 1.0, jax.random.fold_in(key, 6)
    for position, blocks in cuts:
        heights = jnp.exp(jax.random.uniform(jax.random.fold_in(own, position), (blocks,), jnp.float32, low / len(cuts), largest / len(cuts)))
        loudness = loudness * jnp.repeat(heights, dims[position] // blocks).reshape([-1 if axis == position else 1 for axis in range(len(dims))])
    return loudness


def profile(count, total, reach, slope):
    loads = [(1 << 20) // math.isqrt(rank ** slope) + 1 for rank in range(2, count + 1)]
    surplus, holding = total - reach - (count - 1), [1] * (count - 1)
    while surplus > 0:
        free = [i for i in range(count - 1) if holding[i] < reach]
        mass, remaining = sum([loads[i] for i in free]), surplus
        for i in free:
            addition = min(reach - holding[i], max(1, remaining * loads[i] // mass), surplus)
            holding[i] = holding[i] + addition
            surplus = surplus - addition
    return np.array([reach] + holding)


def uneven(key, number_of, total, reach, skew):
    if number_of == 2:
        one = jax.random.randint(key, (), max(1, total - reach), min(reach, total - 1) + 1)
        return jnp.stack([one, total - one])
    sizes = jnp.asarray(profile(number_of, total, reach, skew), jnp.int32)
    pairs = (number_of - 1) // 2
    donor, sink = sizes[1:1 + 2 * pairs:2], sizes[2:2 + 2 * pairs:2]
    slack = jnp.minimum(donor - 1, reach - sink)
    passed = jax.random.randint(jax.random.fold_in(key, 1), (pairs,), 0, 1 << 20) % (slack + 1)
    sizes = sizes.at[1:1 + 2 * pairs:2].set(donor - passed).at[2:2 + 2 * pairs:2].set(sink + passed)
    return sizes[jax.random.permutation(jax.random.fold_in(key, 2), number_of)]


def normal_values(key, shape, deviation, most, cuts=(), kind=jnp.bfloat16):
    gain = shard_levels(key, shape, cuts, -0.22, 0.18) if cuts else 1.0
    result = jax.random.normal(key, shape, jnp.float32) * deviation * gain
    return jnp.minimum(jnp.maximum(result, -most), most).astype(kind)


def setup_inputs(seed: int = 0) -> dict:
    arg_keys = jax.random.split(jax.random.key(seed), 7)
    hidden = normal_values(arg_keys[0], (EXAMPLES, SEQ, FF), 1.0, 6.0, ((0, 4), (2, 128)))
    out_grad = normal_values(arg_keys[1], (EXAMPLES, SEQ, D), (1.5 / SEQ ** 0.5), 0.5625, ((0, 4), (2, 128)))
    example_len = uneven(arg_keys[2], EXAMPLES, EXAMPLES * SEQ // 2, SEQ, 1).astype(jnp.int32)
    sign_bits = plant((jax.random.randint(arg_keys[3], (ROWS_P, D), 0, 2) < 1).astype(jnp.int32), jax.random.fold_in(arg_keys[3], 1), 0, 1)
    kept_rows = plant(jax.random.randint(arg_keys[4], (KEEP,), 0, ROWS_P), jax.random.fold_in(arg_keys[4], 1), 0, ROWS_P - 1).astype(jnp.int32)
    kept_cols = plant(jax.random.randint(arg_keys[5], (KEEP,), 0, D), jax.random.fold_in(arg_keys[5], 1), 0, D - 1).astype(jnp.int32)
    return {"hidden": hidden, "out_grad": out_grad, "example_len": example_len, "sign_bits": sign_bits, "kept_rows": kept_rows, "kept_cols": kept_cols}


def parity_sign(first_bits, second_bits):
    folded = jnp.bitwise_and(first_bits, second_bits)
    for shift_by in (16, 8, 4, 2, 1):
        folded = jnp.bitwise_xor(folded, jnp.right_shift(folded, shift_by))
    return (1 - 2 * jnp.bitwise_and(folded, 1)).astype(jnp.float32)

def sylvester(order):
    positions_all = jnp.arange(order, dtype=jnp.int32)
    return parity_sign(positions_all[:, None], positions_all[None, :])

def reference(hidden, out_grad, example_len, sign_bits, kept_rows, kept_cols):
    rows_blk = FF // N_BLK
    pad_rows = HL // (N_BLK * D)
    low_width = min(D, 128)
    high_width = D // low_width
    top_precision = lax.Precision.HIGHEST
    positions = jnp.arange(SEQ, dtype=jnp.int32)
    token_mask = (positions[None, :] < example_len[:, None]).astype(jnp.bfloat16)
    masked = hidden * token_mask[:, :, None]
    grad_data = out_grad.astype(jnp.float32)
    h_rows = sylvester(pad_rows)[:, :rows_blk]
    h_high = sylvester(high_width)
    h_low = sylvester(low_width)
    kept_block = kept_rows // pad_rows
    kept_pos = kept_rows % pad_rows
    flat_index = (kept_pos * D + kept_cols).astype(jnp.int32)
    sign_all = (1 - 2 * sign_bits).astype(jnp.float32)

    def one_block(acc_total, block_idx):
        part_rows = lax.dynamic_slice_in_dim(masked, block_idx * rows_blk, rows_blk, 2).astype(jnp.float32)
        gradient = jnp.einsum('etr,etd->erd', part_rows, grad_data, precision=top_precision)
        sign_tile = lax.dynamic_slice_in_dim(sign_all, block_idx * pad_rows, rows_blk, 0)
        weighted = gradient * sign_tile[None]
        mixed_vals = jnp.einsum('pr,erd->epd', h_rows, weighted, precision=top_precision)
        mixed_vals = mixed_vals.reshape(EXAMPLES, pad_rows, high_width, low_width)
        mixed_vals = jnp.einsum('ab,epbc->epac', h_high, mixed_vals, precision=top_precision)
        mixed_vals = jnp.einsum('epac,fc->epaf', mixed_vals, h_low, precision=top_precision)
        picked = jnp.take(mixed_vals.reshape(EXAMPLES, pad_rows * D), flat_index, axis=1)
        return (acc_total + picked * parity_sign(kept_block, block_idx)[None, :], None)
    acc_total, _ = lax.scan(one_block, jnp.zeros((EXAMPLES, KEEP), jnp.float32), jnp.arange(N_BLK, dtype=jnp.int32))
    return acc_total / math.sqrt(HL)
```

```python
import functools
import math

import jax
import jax.numpy as jnp
from jax import lax
from jax.experimental import pallas as pl
from jax.experimental.pallas import tpu as pltpu
from jax.sharding import PartitionSpec as P

NY, NZ, NC, NX = 4, 16, 2, 4
NE = 4
TOK = 256
JW = 32
RP = 96
NK = 11
NG = 4
GW = 256
VMEM_MB = 56 << 20
NT = (((1,), (1,)), ((), ()))
TN = (((0,), (0,)), ((), ()))


def parity(bits):
    for shift_by in (16, 8, 4, 2, 1):
        bits = jnp.bitwise_xor(bits, jnp.right_shift(bits, shift_by))
    return jnp.bitwise_and(bits, 1)


def sylvester_tile(rows, cols, row_mask, col_mask):
    a = jnp.bitwise_and(lax.broadcasted_iota(jnp.int32, (rows, cols), 0), row_mask)
    b = jnp.bitwise_and(lax.broadcasted_iota(jnp.int32, (rows, cols), 1), col_mask)
    return (1 - 2 * parity(jnp.bitwise_and(a, b))).astype(jnp.float32)


def split(values):
    hi = values.astype(jnp.bfloat16)
    lo = (values - hi.astype(jnp.float32)).astype(jnp.bfloat16)
    return hi, lo


def device(y, z, c, x):
    return ((y * NZ + z) * NC + c, x)


def place():
    b = lax.axis_index("blk")
    return b // (NZ * NC), (b // NC) % NZ, b % NC, lax.axis_index("ex")


def butterfly(values, width):
    values = list(values) + [None] * (width - len(values))
    step = width // 2
    while step:
        for base in range(0, width, 2 * step):
            for j in range(base, base + step):
                a, b = values[j], values[j + step]
                values[j], values[j + step] = (a, a) if b is None else (a + b, a - b)
        step //= 2
    return values


LINES = 4
CH = LINES * 128
GROUP = 32
KHI = 16


def spread_rows(xs, flat, g):
    def mix(rb, carry):
        rows = pl.ds(pl.multiple_of(rb * 8, 8), 8)
        for p, v in enumerate(butterfly([xs[k, rows, :] for k in range(NK)], KHI)):
            flat[pl.ds(pl.multiple_of((p * NG + g) * GW + rb * 8, 8), 8), :] = v
        return carry

    lax.fori_loop(0, GW // 8, mix, 0)


def join_groups(flat):
    def mix(rb, carry):
        for p in range(KHI):
            rows = [pl.ds(pl.multiple_of((p * NG + g) * GW + rb * 8, 8), 8) for g in range(NG)]
            for g, v in enumerate(butterfly([flat[r, :] for r in rows], NG)):
                flat[rows[g], :] = v
        return carry

    lax.fori_loop(0, GW // 8, mix, 0)


def make_picker(kr_ref, kc_ref, idx_smem, table_ref, out_ref, y, zc, scale):
    row = lax.broadcasted_iota(jnp.int32, (128, 128), 0)
    lane = lax.broadcasted_iota(jnp.int32, (128, 128), 1)
    owner = jnp.bitwise_and((lane >> 5) + y, NY - 1)
    code = row & 31
    bits = jnp.bitwise_or(jnp.bitwise_and(code >> 3, owner) << 3, jnp.bitwise_and(code, lane) & 7)
    hx = (1 - 2 * parity(bits)).astype(jnp.float32)
    hx = jnp.where((row >> 5) == ((lane >> 3) & (NE - 1)), hx, 0.0).astype(jnp.bfloat16)
    weights = jnp.concatenate([hx, hx], axis=1)
    which = lax.broadcasted_iota(jnp.int32, (32, 128), 0)

    def pick(ch, rows_ref):
        for h in range(LINES):
            line = ch * LINES + h
            for g in range(128 // GROUP):
                rows = [table_ref[pl.ds(idx_smem[line, g * GROUP + u], 1), :] for u in range(GROUP)]
                for u in range(GROUP):
                    rows_ref[pl.ds(h * 128 + g * GROUP + u, 1), :] = rows[u]

    def finish(ch, rows_ref):
        parts = []
        for h in range(LINES):
            line = ch * LINES + h
            kr = kr_ref[pl.ds(line, 1), :]
            kc = kc_ref[pl.ds(line, 1), :]
            flips = jnp.bitwise_xor(jnp.bitwise_and((kr >> 7) & 31, zc), jnp.bitwise_and(kc >> 10, y) << 5)
            sign = (1 - 2 * parity(flips)).astype(jnp.float32) * scale
            parts.append(jnp.where(which == ((kr >> 12) << 3) + jnp.bitwise_and(kr, 7), sign, 0.0))
        onehot = jnp.concatenate(parts, axis=1)
        hi, lo = split(rows_ref[...])
        both = jnp.concatenate([hi, lo], axis=1)
        prod = lax.dot_general(weights, both, NT, preferred_element_type=jnp.float32)
        for e in range(NE):
            res = jnp.sum(prod[32 * e:32 * e + 32] * onehot, axis=0, keepdims=True)
            for h in range(LINES):
                out_ref[ch * LINES + h, pl.ds(e, 1), :] = res[:, 128 * h:128 * h + 128]

    return pick, finish


def remote(src, dst, send, recv, target):
    return pltpu.make_async_remote_copy(
        src_ref=src, dst_ref=dst, send_sem=send, recv_sem=recv,
        device_id=target, device_id_type=pl.DeviceIdType.MESH)


def landed(ref, sem):
    pltpu.make_async_copy(ref, ref, sem).wait()


def greet(peers):
    barrier = pltpu.get_barrier_semaphore()
    for peer in peers:
        pl.semaphore_signal(barrier, inc=1, device_id=peer, device_id_type=pl.DeviceIdType.MESH)
    return barrier


def sketch_kernel(own_ref, h_ref, len_ref, sb_ref, krh_ref, kch_ref, out_ref,
                  cols, kr_ref, kc_ref, hin, mall, sall, sout, hbuf, sown, sfor, wbuf, xs, table, rows_a, rows_b, idx_ref, idx_smem,
                  pbuf, ybuf, zsum, zbuf, tbuf, xbuf,
                  r_send, r_recv, p_recv, m_send, m_recv, s_send, s_recv, x_send, x_recv,
                  c_send, c_recv, load_sem, idx_sem, sb_sem, ysend, yrecv, zsend, zrecv, xsend, xrecv, *, scale):
    y, z, c, x = place()
    zpeers = (device(y, (z + 1) % NZ, c, x), device(y, (z + NZ - 1) % NZ, c, x))
    sibling = device(y, z, 1 - c, x)
    ypeers = [device((y + k) % NY, z, c, x) for k in range(1, NY)]
    xpeers = (device(y, z, c, (x + 1) % NX), device(y, z, c, (x + NX - 1) % NX))
    zall = [device(y, (z + k) % NZ, c, x) for k in range(1, NZ)]
    offsets = [(dc, dx) for dx in range(NX) for dc in range(NC) if dc or dx]
    square = [device(y, z, (c + dc) % NC, (x + dx) % NX) for dc, dx in offsets]
    cross = (device(y, (z + 1) % NZ, 1 - c, x), device(y, (z + NZ - 1) % NZ, 1 - c, x))
    peers = list(zpeers) + list(cross) + ypeers + square + zall[1:-1]
    barrier = greet(peers)

    def sign_rows(k):
        width = GW if k else NG * GW
        start = ((y + k) % NY) * (NG * GW) + (x * GW if k else 0)
        src = sb_ref.at[pl.ds(0, RP), pl.ds(pl.multiple_of(start, GW), width)]
        return pltpu.make_async_copy(src, sfor.at[k - 1] if k else sown, sb_sem.at[k])

    loads = [pltpu.make_async_copy(src, dst, load_sem.at[i]) for i, (src, dst) in enumerate((
        (own_ref, cols.at[z, c]), (h_ref, hin), (krh_ref, kr_ref), (kch_ref, kc_ref)))]
    loads[0].start()
    for k in (1, 2, 3):
        sign_rows(k).start()
    for load in loads[1:]:
        load.start()
    sign_rows(0).start()

    def slab(sign, s):
        return (z + NZ - s) % NZ if sign == 0 else (z + s) % NZ

    def ring(sign, half, s, arrival=False):
        part = cols.at[slab(sign, s), c, pl.ds(2 * half, 2)]
        first = isinstance(s, int) and s == 0 and not arrival
        return remote(own_ref.at[pl.ds(2 * half, 2)] if first else part, part, r_send,
                      r_recv.at[sign, half, s if arrival else s + 1], zpeers[sign])

    def last_ring(sign, arrival=False):
        part = cols.at[slab(sign, 8 if arrival else 7), 1 - c if arrival else c, pl.ds(2 * sign, 2)]
        return remote(part, part, c_send, c_recv, cross[sign])

    def pair(sign, s, arrival=False):
        part = cols.at[slab(sign, s), 1 - c if arrival else c]
        return remote(part, part, r_send, p_recv.at[0 if s < 4 else (1 if s < 6 else 2)], sibling)

    def m_copy(side, part, arrival=False):
        there = 3 if side == 0 else 1
        piece = pl.ds(2 * part, 2)
        dst = mall.at[there, piece]
        return remote(dst if arrival else mall.at[0, piece], dst, m_send, m_recv.at[side, 0 if part == side else 1],
                      ypeers[0] if side == 0 else ypeers[2])

    def m_relay(side, arrival=False):
        part = pl.ds(2 * side, 2)
        dst = mall.at[2, part]
        src = mall.at[3 if side == 0 else 1, part]
        return remote(dst if arrival else src, dst, m_send, m_recv.at[2, side],
                      ypeers[0] if side == 0 else ypeers[2])

    def s_copy(k, arrival=False):
        dst = sall.at[NY - k, x]
        return remote(dst if arrival else sout.at[k - 1], dst, s_send, s_recv, ypeers[k - 1])

    def x_copy(side, arrival=False):
        group = x if not arrival else ((x + NX - 1) % NX if side == 0 else (x + 1) % NX)
        part = sall.at[pl.ds(1, NY - 1), group]
        return remote(part, part, x_send, x_recv.at[side], xpeers[side])

    def x_relay(side, arrival=False):
        if arrival:
            group = (x + 2) % NX
        else:
            group = (x + NX - 1) % NX if side == 0 else (x + 1) % NX
        part = sall.at[pl.ds(1, NY - 1), group, pl.ds(side * (RP // 2), RP // 2)]
        return remote(part, part, x_send, x_recv.at[2], xpeers[side])

    def signs(bits):
        return (1 - 2 * bits).astype(jnp.float32).astype(jnp.bfloat16)

    pl.semaphore_wait(barrier, len(peers))
    for half in range(2):
        for sign in range(2):
            ring(sign, half, 0).start()
    loads[0].wait()
    pair(0, 0).start()
    for k in range(1, NY):
        sign_rows(k).wait()
        sout[k - 1] = signs(sfor[k - 1])
        s_copy(k).start()
    loads[1].wait()
    rows_blk = h_ref.shape[0]
    hbuf[0:rows_blk] = hin[...].astype(jnp.float32)
    hbuf[rows_blk:RP] = jnp.zeros((RP - rows_blk, NE, TOK), jnp.float32)
    lane = lax.broadcasted_iota(jnp.int32, (RP, TOK), 1)
    for e in range(NE):
        mall[0, e] = jnp.where(lane < len_ref[e], hbuf[:, e, :], 0.0).astype(jnp.bfloat16)
    for side in range(2):
        m_copy(side, side).start()
    for side in range(2):
        m_copy(side, 1 - side).start()
    loads[2].wait()
    loads[3].wait()
    kpos = jnp.bitwise_and(kr_ref[...], 127)
    idx_ref[...] = (kpos >> 3) * (NG * GW) + jnp.bitwise_and(kc_ref[...], NG * GW - 1)
    to_smem = pltpu.make_async_copy(idx_ref, idx_smem, idx_sem)
    to_smem.start()
    sign_rows(0).wait()
    for g in range(NG):
        sall[0, g] = signs(sown[:, GW * g:GW * g + GW])
    h256 = sylvester_tile(GW, GW, 255, 255).astype(jnp.bfloat16)

    def step(s):
        for half in range(2):
            for sign in range(2):
                ring(sign, half, s, True).wait_recv()
                if s < 7 or half == sign:
                    ring(sign, half, s).start()
                if s == 7 and half == sign:
                    last_ring(sign).start()
        for sign in range(2):
            pair(sign, s).start()

    def compute(g):
        for e in range(NE):
            lhs = mall[:, e].reshape(NY * RP, TOK)
            rhs = cols[pl.ds(NG * g, NG), :, e].reshape(GW, TOK)
            grad = lax.dot_general(lhs, rhs, NT, preferred_element_type=jnp.float32)
            for b in range(NY):
                w = grad[RP * b:RP * b + RP] * sall[b, g].astype(jnp.float32)
                for k in range(NK):
                    wbuf[k, 32 * b + 8 * e:32 * b + 8 * e + 8] = w[8 * k:8 * k + 8]
        for k in range(0, NK, 2):
            n = min(2, NK - k)
            hi, lo = split(wbuf[k:k + n].reshape(128 * n, GW))
            out = (lax.dot_general(h256, hi, NT, preferred_element_type=jnp.float32)
                   + lax.dot_general(h256, lo, NT, preferred_element_type=jnp.float32))
            for i in range(n):
                xs[k + i] = out[:, 128 * i:128 * i + 128]

    step(1)
    step(2)
    landed(sout, s_recv)
    for side in range(2):
        x_copy(side).start()
    step(3)
    step(4)
    for side in range(2):
        m_copy(side, side, True).wait_recv()
        m_relay(side).start()
    for side in range(2):
        x_copy(side, True).wait_recv()
        x_relay(side).start()
    flat = table
    mine = z // NG
    low = z % NG < 2
    early = jnp.where(low, (mine + NG - 1) % NG, (mine + 1) % NG)
    late = jnp.where(low, (mine + 1) % NG, (mine + NG - 1) % NG)

    def stage(t, carry):
        @pl.when(t == 0)
        def _():
            step(5)
            step(6)
            landed(cols.at[pl.ds(0, 7), 0], p_recv.at[0])
            for side in range(2):
                m_copy(side, 1 - side, True).wait_recv()
                m_relay(side, True).wait_recv()
            landed(sall.at[pl.ds(1, NY - 1), 0], x_recv.at[2])

        @pl.when(t == 1)
        def _():
            step(7)
            landed(cols.at[pl.ds(0, 4), 0], p_recv.at[1])

        @pl.when(t == 2)
        def _():
            landed(cols.at[pl.ds(0, 4), 0], p_recv.at[2])

        @pl.when(t == 3)
        def _():
            for sign in range(2):
                ring(sign, sign, 8, True).wait_recv()
            landed(cols.at[0, 0], c_recv)

        g = jnp.where(t == 0, mine, jnp.where(t == 1, early, jnp.where(t == 2, late, (mine + 2) % NG)))
        compute(g)
        spread_rows(xs, flat, g)
        return carry

    lax.fori_loop(0, NG, stage, 0)
    join_groups(flat)
    to_smem.wait()
    pick, finish = make_picker(kr_ref, kc_ref, idx_smem, table, pbuf, y, z * NC + c, scale)
    quarter = pbuf.shape[0] // NY
    per = quarter // LINES

    def y_copy(k):
        far = (y + k) % NY
        return remote(pbuf.at[pl.ds(far * quarter, quarter)], ybuf.at[k - 1], ysend, yrecv,
                      device(far, z, c, x))

    def turn(q):
        return jnp.where(q == 0, 2, jnp.where(q == 1, 1, 3))

    def chunk_at(j):
        other = ((y + turn(j // per)) % NY) * per + j % per
        off = jnp.where(j == 12, 2, jnp.where(j == 13, 1, jnp.where(j == 14, 3, 0)))
        return jnp.where(j < 12, other, y * per + (z // LINES + off) % per)

    def z_copy(k):
        far = (z + k) % NZ
        return remote(zsum.at[far], zbuf.at[k - 1], zsend, zrecv, device(y, far, c, x))

    def add_up(far):
        total = pbuf[y * quarter + far]
        for k in range(1, NY):
            total = total + ybuf[k - 1, far]
        zsum[far] = total

    def emit(j, own):
        first = LINES * (chunk_at(j) - y * per)
        for h in range(LINES):
            far = first + h
            add_up(far)
            if own:
                @pl.when(far != z)
                def _():
                    z_copy((far + NZ - z) % NZ).start()
            else:
                z_copy((far + NZ - z) % NZ).start()

    def drain():
        landed(cols.at[pl.ds(0, NZ - 1)], r_send)
        landed(cols.at[0, 0], c_send)
        landed(mall.at[pl.ds(0, NY - 1)], m_send)
        landed(sout, s_send)
        landed(sall.at[pl.ds(0, 3), pl.ds(0, 3)], x_send)

    pick(chunk_at(0), rows_a)

    def body(n, carry):
        pick(chunk_at(2 * n + 1), rows_b)
        finish(chunk_at(2 * n), rows_a)
        pick(chunk_at(2 * n + 2), rows_a)
        finish(chunk_at(2 * n + 1), rows_b)

        @pl.when((n < 6) & (n % 2 == 1))
        def _():
            y_copy(turn(n // 2)).start()

        @pl.when(n == 6)
        def _():
            landed(ybuf, yrecv)
            emit(12, False)
            emit(13, False)

        return carry

    lax.fori_loop(0, 7, body, 0)
    pick(chunk_at(15), rows_b)
    finish(chunk_at(14), rows_a)
    emit(14, False)
    finish(chunk_at(15), rows_b)
    emit(15, True)
    drain()
    landed(zbuf, zrecv)
    total = zsum[z]
    for k in range(1, NZ):
        total = total + zbuf[k - 1]
    tbuf[...] = total

    def last_copy(i):
        return remote(tbuf, xbuf.at[i], xsend, xrecv, square[i])

    for i in range(len(offsets)):
        last_copy(i).start()
    landed(ybuf, ysend)
    landed(zbuf, zsend)
    landed(xbuf, xrecv)
    slot = {o: i for i, o in enumerate(offsets)}
    for dx in range(NX):
        first = total if dx == 0 else xbuf[slot[(0, dx)]]
        out_ref[(x - dx + NX) % NX] = first + xbuf[slot[(1, dx)]]

    landed(xbuf, xsend)


def local(hidden, out_grad, example_len, sign_bits, kept_rows, kept_cols):
    keep = kept_rows.shape[0]
    total_len = sign_bits.shape[0] * lax.axis_size("blk") * sign_bits.shape[1]
    blk_index = lax.axis_index("blk")
    dma = pltpu.SemaphoreType.DMA
    vm = pl.BlockSpec(memory_space=pltpu.VMEM)
    hbm = pl.BlockSpec(memory_space=pl.ANY)

    f32 = jnp.float32
    blocks = pl.pallas_call(
        functools.partial(sketch_kernel, scale=1.0 / math.sqrt(total_len)),
        out_shape=jax.ShapeDtypeStruct((NX, NE, 128), f32),
        in_specs=[hbm, hbm, pl.BlockSpec(memory_space=pltpu.SMEM), hbm, hbm, hbm],
        out_specs=vm,
        scratch_shapes=[
            pltpu.VMEM((NZ, NC, NE, JW, TOK), jnp.bfloat16),
            pltpu.VMEM((keep // 128, 128), jnp.int32), pltpu.VMEM((keep // 128, 128), jnp.int32),
            pltpu.VMEM((hidden.shape[2], NE, TOK), jnp.bfloat16),
            pltpu.VMEM((NY, NE, RP, TOK), jnp.bfloat16),
            pltpu.VMEM((NY, NG, RP, GW), jnp.bfloat16),
            pltpu.VMEM((NY - 1, RP, GW), jnp.bfloat16),
            pltpu.VMEM((RP, NE, TOK), f32),
            pltpu.VMEM((RP, NG * GW), jnp.int32),
            pltpu.VMEM((NY - 1, RP, GW), jnp.int32),
            pltpu.VMEM((NK, 128, GW), f32),
            pltpu.VMEM((NK, GW, 128), f32),
            pltpu.VMEM((KHI * NG * GW, 128), f32),
            pltpu.VMEM((CH, 128), f32), pltpu.VMEM((CH, 128), f32),
            pltpu.VMEM((keep // 128, 128), jnp.int32), pltpu.SMEM((keep // 128, 128), jnp.int32),
            pltpu.VMEM((keep // 128, NE, 128), f32),
            pltpu.VMEM((NY - 1, NZ, NE, 128), f32),
            pltpu.VMEM((NZ, NE, 128), f32),
            pltpu.VMEM((NZ - 1, NE, 128), f32),
            pltpu.VMEM((NE, 128), f32),
            pltpu.VMEM((7, NE, 128), f32),
            dma, dma((2, 2, 9)), dma((3,)), dma, dma((3, 2)),
            dma, dma, dma, dma((3,)),
            dma, dma, dma((4,)), dma, dma((NY,)), dma, dma, dma, dma, dma, dma,
        ],
        compiler_params=pltpu.CompilerParams(
            collective_id=0, has_side_effects=True, vmem_limit_bytes=VMEM_MB),
    )(out_grad.transpose(0, 2, 1), hidden.transpose(2, 0, 1), example_len, sign_bits,
      kept_rows.reshape(keep // 128, 128), kept_cols.reshape(keep // 128, 128))
    start = (blk_index % NC) * 64 + lax.axis_index("ex") * 16
    return lax.dynamic_slice_in_dim(blocks.reshape(4 * NE, 128), start, 16, axis=1)


def solution(mesh):
    return jax.shard_map(
        local,
        mesh=mesh,
        in_specs=(P("ex", None, "blk"), P("ex", None, "blk"), P("ex"), P("blk", None), P(), P()),
        out_specs=P(None, ("blk", "ex")),
        check_vma=False,
    )
```

```python
import functools
import math

import jax
import jax.numpy as jnp
from jax import lax
from jax.experimental import pallas as pl
from jax.experimental.pallas import tpu as pltpu
from jax.sharding import PartitionSpec as P

NY, NZ, NC, NX = 4, 16, 2, 4
NE = 4
TOK = 256
JW = 32
RP = 96
NK = 11
NG = 4
GW = 256
VMEM_MB = 56 << 20
NT = (((1,), (1,)), ((), ()))
TN = (((0,), (0,)), ((), ()))


def parity(bits):
    for shift_by in (16, 8, 4, 2, 1):
        bits = jnp.bitwise_xor(bits, jnp.right_shift(bits, shift_by))
    return jnp.bitwise_and(bits, 1)


def sylvester_tile(rows, cols, row_mask, col_mask):
    a = jnp.bitwise_and(lax.broadcasted_iota(jnp.int32, (rows, cols), 0), row_mask)
    b = jnp.bitwise_and(lax.broadcasted_iota(jnp.int32, (rows, cols), 1), col_mask)
    return (1 - 2 * parity(jnp.bitwise_and(a, b))).astype(jnp.float32)


def split(values):
    hi = values.astype(jnp.bfloat16)
    lo = (values - hi.astype(jnp.float32)).astype(jnp.bfloat16)
    return hi, lo


def device(y, z, c, x):
    return ((y * NZ + z) * NC + c, x)


def place():
    b = lax.axis_index("blk")
    return b // (NZ * NC), (b // NC) % NZ, b % NC, lax.axis_index("ex")


def butterfly(values, width):
    values = list(values) + [None] * (width - len(values))
    step = width // 2
    while step:
        for base in range(0, width, 2 * step):
            for j in range(base, base + step):
                a, b = values[j], values[j + step]
                values[j], values[j + step] = (a, a) if b is None else (a + b, a - b)
        step //= 2
    return values


LINES = 4
CH = LINES * 128
GROUP = 32
KHI = 16


def spread_rows(xs, flat, g):
    def mix(rb, carry):
        rows = pl.ds(pl.multiple_of(rb * 8, 8), 8)
        for p, v in enumerate(butterfly([xs[k, rows, :] for k in range(NK)], KHI)):
            flat[pl.ds(pl.multiple_of((p * NG + g) * GW + rb * 8, 8), 8), :] = v
        return carry

    lax.fori_loop(0, GW // 8, mix, 0, unroll=4)


def join_groups(flat):
    def mix(rb, carry):
        for p in range(KHI):
            rows = [pl.ds(pl.multiple_of((p * NG + g) * GW + rb * 8, 8), 8) for g in range(NG)]
            for g, v in enumerate(butterfly([flat[r, :] for r in rows], NG)):
                flat[rows[g], :] = v
        return carry

    lax.fori_loop(0, GW // 8, mix, 0, unroll=2)


def make_picker(kr_ref, kc_ref, idx_smem, table_ref, out_ref, y, zc, scale):
    row = lax.broadcasted_iota(jnp.int32, (128, 128), 0)
    lane = lax.broadcasted_iota(jnp.int32, (128, 128), 1)
    owner = jnp.bitwise_and((lane >> 5) + y, NY - 1)
    code = row & 31
    bits = jnp.bitwise_or(jnp.bitwise_and(code >> 3, owner) << 3, jnp.bitwise_and(code, lane) & 7)
    hx = (1 - 2 * parity(bits)).astype(jnp.float32)
    hx = jnp.where((row >> 5) == ((lane >> 3) & (NE - 1)), hx, 0.0).astype(jnp.bfloat16)
    weights = jnp.concatenate([hx, hx], axis=1)
    which = lax.broadcasted_iota(jnp.int32, (32, 128), 0)

    def pick(ch, rows_ref):
        for h in range(LINES):
            line = ch * LINES + h
            for g in range(128 // GROUP):
                rows = [table_ref[pl.ds(idx_smem[line, g * GROUP + u], 1), :] for u in range(GROUP)]
                for u in range(GROUP):
                    rows_ref[pl.ds(h * 128 + g * GROUP + u, 1), :] = rows[u]

    def finish(ch, rows_ref):
        parts = []
        for h in range(LINES):
            line = ch * LINES + h
            kr = kr_ref[pl.ds(line, 1), :]
            kc = kc_ref[pl.ds(line, 1), :]
            flips = jnp.bitwise_xor(jnp.bitwise_and((kr >> 7) & 31, zc), jnp.bitwise_and(kc >> 10, y) << 5)
            sign = (1 - 2 * parity(flips)).astype(jnp.float32) * scale
            parts.append(jnp.where(which == ((kr >> 12) << 3) + jnp.bitwise_and(kr, 7), sign, 0.0))
        onehot = jnp.concatenate(parts, axis=1)
        hi, lo = split(rows_ref[...])
        both = jnp.concatenate([hi, lo], axis=1)
        prod = lax.dot_general(weights, both, NT, preferred_element_type=jnp.float32)
        for e in range(NE):
            res = jnp.sum(prod[32 * e:32 * e + 32] * onehot, axis=0, keepdims=True)
            for h in range(LINES):
                out_ref[ch * LINES + h, pl.ds(e, 1), :] = res[:, 128 * h:128 * h + 128]

    return pick, finish


def remote(src, dst, send, recv, target):
    return pltpu.make_async_remote_copy(
        src_ref=src, dst_ref=dst, send_sem=send, recv_sem=recv,
        device_id=target, device_id_type=pl.DeviceIdType.MESH)


def landed(ref, sem):
    pltpu.make_async_copy(ref, ref, sem).wait()


def greet(peers):
    barrier = pltpu.get_barrier_semaphore()
    for peer in peers:
        pl.semaphore_signal(barrier, inc=1, device_id=peer, device_id_type=pl.DeviceIdType.MESH)
    return barrier


def sketch_kernel(own_ref, h_ref, len_ref, sb_ref, krh_ref, kch_ref, out_ref,
                  cols, kr_ref, kc_ref, hin, mall, sall, sout, hbuf, sown, sfor, wbuf, xs, table, rows_a, rows_b, idx_ref, idx_smem,
                  pbuf, ybuf, zsum, zbuf, tbuf, xbuf,
                  r_send, r_recv, p_recv, m_send, m_recv, s_send, s_recv, x_send, x_recv,
                  c_send, c_recv, load_sem, idx_sem, sb_sem, ysend, yrecv, zsend, zrecv, xsend, xrecv, *, scale):
    y, z, c, x = place()
    zpeers = (device(y, (z + 1) % NZ, c, x), device(y, (z + NZ - 1) % NZ, c, x))
    sibling = device(y, z, 1 - c, x)
    ypeers = [device((y + k) % NY, z, c, x) for k in range(1, NY)]
    xpeers = (device(y, z, c, (x + 1) % NX), device(y, z, c, (x + NX - 1) % NX))
    zall = [device(y, (z + k) % NZ, c, x) for k in range(1, NZ)]
    offsets = [(dc, dx) for dx in range(NX) for dc in range(NC) if dc or dx]
    square = [device(y, z, (c + dc) % NC, (x + dx) % NX) for dc, dx in offsets]
    cross = (device(y, (z + 1) % NZ, 1 - c, x), device(y, (z + NZ - 1) % NZ, 1 - c, x))
    peers = list(zpeers) + list(cross) + ypeers + square + zall[1:-1]
    barrier = greet(peers)

    def sign_rows(k):
        width = GW if k else NG * GW
        start = ((y + k) % NY) * (NG * GW) + (x * GW if k else 0)
        src = sb_ref.at[pl.ds(0, RP), pl.ds(pl.multiple_of(start, GW), width)]
        return pltpu.make_async_copy(src, sfor.at[k - 1] if k else sown, sb_sem.at[k])

    loads = [pltpu.make_async_copy(src, dst, load_sem.at[i]) for i, (src, dst) in enumerate((
        (own_ref, cols.at[z, c]), (h_ref, hin), (krh_ref, kr_ref), (kch_ref, kc_ref)))]
    loads[0].start()
    for k in (1, 2, 3):
        sign_rows(k).start()
    for load in loads[1:]:
        load.start()
    sign_rows(0).start()

    def slab(sign, s):
        return (z + NZ - s) % NZ if sign == 0 else (z + s) % NZ

    def ring(sign, half, s, arrival=False):
        part = cols.at[slab(sign, s), c, half]
        first = isinstance(s, int) and s == 0 and not arrival
        return remote(own_ref.at[half] if first else part, part, r_send,
                      r_recv.at[sign, half, s if arrival else s + 1], zpeers[sign])

    def last_ring(sign, arrival=False):
        part = cols.at[slab(sign, 8 if arrival else 7), 1 - c if arrival else c, pl.ds(2 * sign, 2)]
        return remote(part, part, c_send, c_recv, cross[sign])

    def pair(sign, s, arrival=False):
        part = cols.at[slab(sign, s), 1 - c if arrival else c]
        return remote(part, part, r_send, p_recv.at[0 if s < 4 else (1 if s < 6 else 2)], sibling)

    def m_copy(side, part, arrival=False):
        there = 3 if side == 0 else 1
        piece = pl.ds(2 * part, 2)
        dst = mall.at[there, piece]
        return remote(dst if arrival else mall.at[0, piece], dst, m_send, m_recv.at[side, 0 if part == side else 1],
                      ypeers[0] if side == 0 else ypeers[2])

    def m_relay(side, arrival=False):
        part = pl.ds(2 * side, 2)
        dst = mall.at[2, part]
        src = mall.at[3 if side == 0 else 1, part]
        return remote(dst if arrival else src, dst, m_send, m_recv.at[2, side],
                      ypeers[0] if side == 0 else ypeers[2])

    def s_copy(k, arrival=False):
        dst = sall.at[NY - k, x]
        return remote(dst if arrival else sout.at[k - 1], dst, s_send, s_recv, ypeers[k - 1])

    def x_copy(side, arrival=False):
        group = x if not arrival else ((x + NX - 1) % NX if side == 0 else (x + 1) % NX)
        part = sall.at[pl.ds(1, NY - 1), group]
        return remote(part, part, x_send, x_recv.at[side], xpeers[side])

    def x_relay(side, arrival=False):
        if arrival:
            group = (x + 2) % NX
        else:
            group = (x + NX - 1) % NX if side == 0 else (x + 1) % NX
        part = sall.at[pl.ds(1, NY - 1), group, pl.ds(side * (RP // 2), RP // 2)]
        return remote(part, part, x_send, x_recv.at[2], xpeers[side])

    def signs(bits):
        return (1 - 2 * bits).astype(jnp.float32).astype(jnp.bfloat16)

    pl.semaphore_wait(barrier, len(peers))
    for half in range(NE):
        for sign in range(2):
            ring(sign, half, 0).start()
    loads[0].wait()
    pair(0, 0).start()
    for k in range(1, NY):
        sign_rows(k).wait()
        sout[k - 1] = signs(sfor[k - 1])
        s_copy(k).start()
    loads[1].wait()
    rows_blk = h_ref.shape[0]
    hbuf[0:rows_blk] = hin[...].astype(jnp.float32)
    hbuf[rows_blk:RP] = jnp.zeros((RP - rows_blk, NE, TOK), jnp.float32)
    lane = lax.broadcasted_iota(jnp.int32, (RP, TOK), 1)
    for e in range(NE):
        mall[0, e] = jnp.where(lane < len_ref[e], hbuf[:, e, :], 0.0).astype(jnp.bfloat16)
    for side in range(2):
        m_copy(side, side).start()
    for side in range(2):
        m_copy(side, 1 - side).start()
    loads[2].wait()
    loads[3].wait()
    kpos = jnp.bitwise_and(kr_ref[...], 127)
    idx_ref[...] = (kpos >> 3) * (NG * GW) + jnp.bitwise_and(kc_ref[...], NG * GW - 1)
    to_smem = pltpu.make_async_copy(idx_ref, idx_smem, idx_sem)
    to_smem.start()
    sign_rows(0).wait()
    for g in range(NG):
        sall[0, g] = signs(sown[:, GW * g:GW * g + GW])
    h256 = sylvester_tile(GW, GW, 255, 255).astype(jnp.bfloat16)

    def step(s):
        for half in range(NE):
            for sign in range(2):
                ring(sign, half, s, True).wait_recv()
                if s < 7 or half // 2 == sign:
                    ring(sign, half, s).start()
        if s == 7:
            for sign in range(2):
                last_ring(sign).start()
        for sign in range(2):
            pair(sign, s).start()

    def compute(g):
        for e in range(NE):
            lhs = mall[:, e].reshape(NY * RP, TOK)
            rhs = cols[pl.ds(NG * g, NG), :, e].reshape(GW, TOK)
            grad = lax.dot_general(lhs, rhs, NT, preferred_element_type=jnp.float32)
            for b in range(NY):
                w = grad[RP * b:RP * b + RP] * sall[b, g].astype(jnp.float32)
                for k in range(NK):
                    wbuf[k, 32 * b + 8 * e:32 * b + 8 * e + 8] = w[8 * k:8 * k + 8]
        for k in range(0, NK, 2):
            n = min(2, NK - k)
            hi, lo = split(wbuf[k:k + n].reshape(128 * n, GW))
            out = (lax.dot_general(h256, hi, NT, preferred_element_type=jnp.float32)
                   + lax.dot_general(h256, lo, NT, preferred_element_type=jnp.float32))
            for i in range(n):
                xs[k + i] = out[:, 128 * i:128 * i + 128]

    step(1)
    step(2)
    landed(sout, s_recv)
    for side in range(2):
        x_copy(side).start()
    step(3)
    step(4)
    for side in range(2):
        m_copy(side, side, True).wait_recv()
        m_relay(side).start()
    for side in range(2):
        x_copy(side, True).wait_recv()
        x_relay(side).start()
    flat = table
    mine = z // NG
    low = z % NG < 2
    early = jnp.where(low, (mine + NG - 1) % NG, (mine + 1) % NG)
    late = jnp.where(low, (mine + 1) % NG, (mine + NG - 1) % NG)

    def stage(t, carry):
        @pl.when(t == 0)
        def _():
            step(5)
            step(6)
            landed(cols.at[pl.ds(0, 7), 0], p_recv.at[0])
            for side in range(2):
                m_copy(side, 1 - side, True).wait_recv()
                m_relay(side, True).wait_recv()
            landed(sall.at[pl.ds(1, NY - 1), 0], x_recv.at[2])

        @pl.when(t == 1)
        def _():
            step(7)
            landed(cols.at[pl.ds(0, 4), 0], p_recv.at[1])

        @pl.when(t == 2)
        def _():
            landed(cols.at[pl.ds(0, 4), 0], p_recv.at[2])

        @pl.when(t == 3)
        def _():
            for sign in range(2):
                for half in (2 * sign, 2 * sign + 1):
                    ring(sign, half, 8, True).wait_recv()
            landed(cols.at[0, 0], c_recv)

        g = jnp.where(t == 0, mine, jnp.where(t == 1, early, jnp.where(t == 2, late, (mine + 2) % NG)))
        compute(g)
        spread_rows(xs, flat, g)
        return carry

    lax.fori_loop(0, NG, stage, 0)
    join_groups(flat)
    to_smem.wait()
    pick, finish = make_picker(kr_ref, kc_ref, idx_smem, table, pbuf, y, z * NC + c, scale)
    quarter = pbuf.shape[0] // NY
    per = quarter // LINES

    def y_copy(k):
        far = (y + k) % NY
        return remote(pbuf.at[pl.ds(far * quarter, quarter)], ybuf.at[k - 1], ysend, yrecv,
                      device(far, z, c, x))

    def turn(q):
        return jnp.where(q == 0, 2, jnp.where(q == 1, 1, 3))

    def chunk_at(j):
        other = ((y + turn(j // per)) % NY) * per + j % per
        off = jnp.where(j == 12, 2, jnp.where(j == 13, 1, jnp.where(j == 14, 3, 0)))
        return jnp.where(j < 12, other, y * per + (z // LINES + off) % per)

    def z_copy(k):
        far = (z + k) % NZ
        return remote(zsum.at[far], zbuf.at[k - 1], zsend, zrecv, device(y, far, c, x))

    def add_up(far):
        total = pbuf[y * quarter + far]
        for k in range(1, NY):
            total = total + ybuf[k - 1, far]
        zsum[far] = total

    def emit(j, own):
        first = LINES * (chunk_at(j) - y * per)
        for h in range(LINES):
            far = first + h
            add_up(far)
            if own:
                @pl.when(far != z)
                def _():
                    z_copy((far + NZ - z) % NZ).start()
            else:
                z_copy((far + NZ - z) % NZ).start()

    def drain():
        landed(cols.at[pl.ds(0, NZ - 1)], r_send)
        landed(cols.at[0, 0], c_send)
        landed(mall.at[pl.ds(0, NY - 1)], m_send)
        landed(sout, s_send)
        landed(sall.at[pl.ds(0, 3), pl.ds(0, 3)], x_send)

    pick(chunk_at(0), rows_a)

    def body(n, carry):
        pick(chunk_at(2 * n + 1), rows_b)
        finish(chunk_at(2 * n), rows_a)
        pick(chunk_at(2 * n + 2), rows_a)
        finish(chunk_at(2 * n + 1), rows_b)

        @pl.when((n < 6) & (n % 2 == 1))
        def _():
            y_copy(turn(n // 2)).start()

        @pl.when(n == 6)
        def _():
            landed(ybuf, yrecv)
            emit(12, False)
            emit(13, False)

        return carry

    lax.fori_loop(0, 7, body, 0)
    pick(chunk_at(15), rows_b)
    finish(chunk_at(14), rows_a)
    emit(14, False)
    finish(chunk_at(15), rows_b)
    emit(15, True)
    drain()
    landed(zbuf, zrecv)
    total = zsum[z]
    for k in range(1, NZ):
        total = total + zbuf[k - 1]
    tbuf[...] = total

    def last_copy(i):
        return remote(tbuf, xbuf.at[i], xsend, xrecv, square[i])

    for i in range(len(offsets)):
        last_copy(i).start()
    landed(ybuf, ysend)
    landed(zbuf, zsend)
    landed(xbuf, xrecv)
    slot = {o: i for i, o in enumerate(offsets)}
    for dx in range(NX):
        first = total if dx == 0 else xbuf[slot[(0, dx)]]
        out_ref[(x - dx + NX) % NX] = first + xbuf[slot[(1, dx)]]

    landed(xbuf, xsend)


def local(hidden, out_grad, example_len, sign_bits, kept_rows, kept_cols):
    keep = kept_rows.shape[0]
    total_len = sign_bits.shape[0] * lax.axis_size("blk") * sign_bits.shape[1]
    blk_index = lax.axis_index("blk")
    dma = pltpu.SemaphoreType.DMA
    vm = pl.BlockSpec(memory_space=pltpu.VMEM)
    hbm = pl.BlockSpec(memory_space=pl.ANY)

    f32 = jnp.float32
    blocks = pl.pallas_call(
        functools.partial(sketch_kernel, scale=1.0 / math.sqrt(total_len)),
        out_shape=jax.ShapeDtypeStruct((NX, NE, 128), f32),
        in_specs=[hbm, hbm, pl.BlockSpec(memory_space=pltpu.SMEM), hbm, hbm, hbm],
        out_specs=vm,
        scratch_shapes=[
            pltpu.VMEM((NZ, NC, NE, JW, TOK), jnp.bfloat16),
            pltpu.VMEM((keep // 128, 128), jnp.int32), pltpu.VMEM((keep // 128, 128), jnp.int32),
            pltpu.VMEM((hidden.shape[2], NE, TOK), jnp.bfloat16),
            pltpu.VMEM((NY, NE, RP, TOK), jnp.bfloat16),
            pltpu.VMEM((NY, NG, RP, GW), jnp.bfloat16),
            pltpu.VMEM((NY - 1, RP, GW), jnp.bfloat16),
            pltpu.VMEM((RP, NE, TOK), f32),
            pltpu.VMEM((RP, NG * GW), jnp.int32),
            pltpu.VMEM((NY - 1, RP, GW), jnp.int32),
            pltpu.VMEM((NK, 128, GW), f32),
            pltpu.VMEM((NK, GW, 128), f32),
            pltpu.VMEM((KHI * NG * GW, 128), f32),
            pltpu.VMEM((CH, 128), f32), pltpu.VMEM((CH, 128), f32),
            pltpu.VMEM((keep // 128, 128), jnp.int32), pltpu.SMEM((keep // 128, 128), jnp.int32),
            pltpu.VMEM((keep // 128, NE, 128), f32),
            pltpu.VMEM((NY - 1, NZ, NE, 128), f32),
            pltpu.VMEM((NZ, NE, 128), f32),
            pltpu.VMEM((NZ - 1, NE, 128), f32),
            pltpu.VMEM((NE, 128), f32),
            pltpu.VMEM((7, NE, 128), f32),
            dma, dma((2, NE, 9)), dma((3,)), dma, dma((3, 2)),
            dma, dma, dma, dma((3,)),
            dma, dma, dma((4,)), dma, dma((NY,)), dma, dma, dma, dma, dma, dma,
        ],
        compiler_params=pltpu.CompilerParams(
            collective_id=0, has_side_effects=True, vmem_limit_bytes=VMEM_MB),
    )(out_grad.transpose(0, 2, 1), hidden.transpose(2, 0, 1), example_len, sign_bits,
      kept_rows.reshape(keep // 128, 128), kept_cols.reshape(keep // 128, 128))
    start = (blk_index % NC) * 64 + lax.axis_index("ex") * 16
    return lax.dynamic_slice_in_dim(blocks.reshape(4 * NE, 128), start, 16, axis=1)


def solution(mesh):
    return jax.shard_map(
        local,
        mesh=mesh,
        in_specs=(P("ex", None, "blk"), P("ex", None, "blk"), P("ex"), P("blk", None), P(), P()),
        out_specs=P(None, ("blk", "ex")),
        check_vma=False,
    )
```

```python
import functools
import math

import jax
import jax.numpy as jnp
from jax import lax
from jax.experimental import pallas as pl
from jax.experimental.pallas import tpu as pltpu
from jax.sharding import PartitionSpec as P

NY, NZ, NC, NX = 4, 16, 2, 4
NE = 4
TOK = 256
JW = 32
RP = 96
NK = 11
NG = 4
GW = 256
VMEM_MB = 56 << 20
NT = (((1,), (1,)), ((), ()))
TN = (((0,), (0,)), ((), ()))


def parity(bits):
    for shift_by in (16, 8, 4, 2, 1):
        bits = jnp.bitwise_xor(bits, jnp.right_shift(bits, shift_by))
    return jnp.bitwise_and(bits, 1)


def sylvester_tile(rows, cols, row_mask, col_mask):
    a = jnp.bitwise_and(lax.broadcasted_iota(jnp.int32, (rows, cols), 0), row_mask)
    b = jnp.bitwise_and(lax.broadcasted_iota(jnp.int32, (rows, cols), 1), col_mask)
    return (1 - 2 * parity(jnp.bitwise_and(a, b))).astype(jnp.float32)


def split(values):
    hi = values.astype(jnp.bfloat16)
    lo = (values - hi.astype(jnp.float32)).astype(jnp.bfloat16)
    return hi, lo


def device(y, z, c, x):
    return ((y * NZ + z) * NC + c, x)


def place():
    b = lax.axis_index("blk")
    return b // (NZ * NC), (b // NC) % NZ, b % NC, lax.axis_index("ex")


def butterfly(values, width):
    values = list(values) + [None] * (width - len(values))
    step = width // 2
    while step:
        for base in range(0, width, 2 * step):
            for j in range(base, base + step):
                a, b = values[j], values[j + step]
                values[j], values[j + step] = (a, a) if b is None else (a + b, a - b)
        step //= 2
    return values


LINES = 4
CH = LINES * 128
GROUP = 32
KHI = 16


def spread_rows(xs, flat, g):
    def mix(rb, carry):
        rows = pl.ds(pl.multiple_of(rb * 8, 8), 8)
        for p, v in enumerate(butterfly([xs[k, rows, :] for k in range(NK)], KHI)):
            flat[pl.ds(pl.multiple_of((p * NG + g) * GW + rb * 8, 8), 8), :] = v
        return carry

    lax.fori_loop(0, GW // 8, mix, 0, unroll=4)


def join_groups(flat):
    def mix(rb, carry):
        for p in range(KHI):
            rows = [pl.ds(pl.multiple_of((p * NG + g) * GW + rb * 8, 8), 8) for g in range(NG)]
            for g, v in enumerate(butterfly([flat[r, :] for r in rows], NG)):
                flat[rows[g], :] = v
        return carry

    lax.fori_loop(0, GW // 8, mix, 0, unroll=2)


def make_picker(kr_ref, kc_ref, idx_smem, table_ref, out_ref, hot, wpick, y, zc, scale):
    row = lax.broadcasted_iota(jnp.int32, (128, 128), 0)
    lane = lax.broadcasted_iota(jnp.int32, (128, 128), 1)
    owner = jnp.bitwise_and((lane >> 5) + y, NY - 1)
    code = row & 31
    bits = jnp.bitwise_or(jnp.bitwise_and(code >> 3, owner) << 3, jnp.bitwise_and(code, lane) & 7)
    hx = (1 - 2 * parity(bits)).astype(jnp.float32)
    hx = jnp.where((row >> 5) == ((lane >> 3) & (NE - 1)), hx, 0.0).astype(jnp.bfloat16)
    wpick[...] = jnp.concatenate([hx, hx], axis=1)
    which = lax.broadcasted_iota(jnp.int32, (32, 128), 0)

    def prepare(line, carry):
        kr = kr_ref[pl.ds(line, 1), :]
        kc = kc_ref[pl.ds(line, 1), :]
        flips = jnp.bitwise_xor(jnp.bitwise_and((kr >> 7) & 31, zc), jnp.bitwise_and(kc >> 10, y) << 5)
        sign = (1 - 2 * parity(flips)).astype(jnp.float32) * scale
        hot[line] = jnp.where(which == ((kr >> 12) << 3) + jnp.bitwise_and(kr, 7), sign, 0.0)
        return carry

    lax.fori_loop(0, kr_ref.shape[0], prepare, 0, unroll=4)

    def pick(ch, rows_ref):
        for h in range(LINES):
            line = ch * LINES + h
            for g in range(128 // GROUP):
                rows = [table_ref[pl.ds(idx_smem[line, g * GROUP + u], 1), :] for u in range(GROUP)]
                for u in range(GROUP):
                    rows_ref[pl.ds(h * 128 + g * GROUP + u, 1), :] = rows[u]

    def finish(ch, rows_ref):
        onehot = jnp.concatenate([hot[ch * LINES + h] for h in range(LINES)], axis=1)
        hi, lo = split(rows_ref[...])
        both = jnp.concatenate([hi, lo], axis=1)
        prod = lax.dot_general(wpick[...], both, NT, preferred_element_type=jnp.float32)
        for e in range(NE):
            res = jnp.sum(prod[32 * e:32 * e + 32] * onehot, axis=0, keepdims=True)
            for h in range(LINES):
                out_ref[ch * LINES + h, pl.ds(e, 1), :] = res[:, 128 * h:128 * h + 128]

    return pick, finish


def remote(src, dst, send, recv, target):
    return pltpu.make_async_remote_copy(
        src_ref=src, dst_ref=dst, send_sem=send, recv_sem=recv,
        device_id=target, device_id_type=pl.DeviceIdType.MESH)


def landed(ref, sem):
    pltpu.make_async_copy(ref, ref, sem).wait()


def greet(peers):
    barrier = pltpu.get_barrier_semaphore()
    for peer in peers:
        pl.semaphore_signal(barrier, inc=1, device_id=peer, device_id_type=pl.DeviceIdType.MESH)
    return barrier


def sketch_kernel(own_ref, h_ref, len_ref, sb_ref, krh_ref, kch_ref, out_ref,
                  cols, kr_ref, kc_ref, hin, mall, sall, sout, hbuf, sown, sfor, wbuf, xs, table, rows_a, rows_b, hot, wpick, idx_ref, idx_smem,
                  pbuf, ybuf, zsum, zbuf, tbuf, xbuf,
                  r_send, r_recv, p_recv, m_send, m_recv, s_send, s_recv, x_send, x_recv, xr_recv,
                  c_send, c_recv, load_sem, idx_sem, sb_sem, ysend, yrecv, zsend, zrecv, xsend, xrecv, *, scale):
    y, z, c, x = place()
    zpeers = (device(y, (z + 1) % NZ, c, x), device(y, (z + NZ - 1) % NZ, c, x))
    sibling = device(y, z, 1 - c, x)
    ypeers = [device((y + k) % NY, z, c, x) for k in range(1, NY)]
    xpeers = (device(y, z, c, (x + 1) % NX), device(y, z, c, (x + NX - 1) % NX))
    zall = [device(y, (z + k) % NZ, c, x) for k in range(1, NZ)]
    offsets = [(dc, dx) for dx in range(NX) for dc in range(NC) if dc or dx]
    square = [device(y, z, (c + dc) % NC, (x + dx) % NX) for dc, dx in offsets]
    cross = (device(y, (z + 1) % NZ, 1 - c, x), device(y, (z + NZ - 1) % NZ, 1 - c, x))
    peers = list(zpeers) + list(cross) + ypeers + square + zall[1:-1]
    barrier = greet(peers)

    def sign_rows(k):
        width = GW if k else NG * GW
        start = ((y + k) % NY) * (NG * GW) + (x * GW if k else 0)
        src = sb_ref.at[pl.ds(0, RP), pl.ds(pl.multiple_of(start, GW), width)]
        return pltpu.make_async_copy(src, sfor.at[k - 1] if k else sown, sb_sem.at[k])

    loads = [pltpu.make_async_copy(src, dst, load_sem.at[i]) for i, (src, dst) in enumerate((
        (own_ref, cols.at[z, c]), (h_ref, hin), (krh_ref, kr_ref), (kch_ref, kc_ref)))]
    loads[0].start()
    for k in (1, 2, 3):
        sign_rows(k).start()
    for load in loads[1:]:
        load.start()
    sign_rows(0).start()

    def slab(sign, s):
        return (z + NZ - s) % NZ if sign == 0 else (z + s) % NZ

    def ring(sign, half, s, arrival=False):
        part = cols.at[slab(sign, s), c, half]
        first = isinstance(s, int) and s == 0 and not arrival
        return remote(own_ref.at[half] if first else part, part, r_send,
                      r_recv.at[sign, half, s if arrival else s + 1], zpeers[sign])

    def last_ring(sign, arrival=False):
        part = cols.at[slab(sign, 8 if arrival else 7), 1 - c if arrival else c, pl.ds(2 * sign, 2)]
        return remote(part, part, c_send, c_recv, cross[sign])

    def pair(sign, s, arrival=False):
        part = cols.at[slab(sign, s), 1 - c if arrival else c]
        return remote(part, part, r_send, p_recv.at[0 if s < 4 else (1 if s < 6 else 2)], sibling)

    def m_copy(side, part, arrival=False):
        there = 3 if side == 0 else 1
        piece = pl.ds(2 * part, 2)
        dst = mall.at[there, piece]
        return remote(dst if arrival else mall.at[0, piece], dst, m_send, m_recv.at[side, 0 if part == side else 1],
                      ypeers[0] if side == 0 else ypeers[2])

    def m_relay(side, arrival=False):
        part = pl.ds(2 * side, 2)
        dst = mall.at[2, part]
        src = mall.at[3 if side == 0 else 1, part]
        return remote(dst if arrival else src, dst, m_send, m_recv.at[2, side],
                      ypeers[0] if side == 0 else ypeers[2])

    def s_copy(k, arrival=False):
        dst = sall.at[NY - k, x]
        return remote(dst if arrival else sout.at[k - 1], dst, s_send, s_recv.at[k - 1], ypeers[k - 1])

    def x_copy(side, k, arrival=False):
        group = x if not arrival else ((x + NX - 1) % NX if side == 0 else (x + 1) % NX)
        part = sall.at[k, group]
        return remote(part, part, x_send, x_recv.at[side, k - 1], xpeers[side])

    def x_relay(side, k):
        group = (x + NX - 1) % NX if side == 0 else (x + 1) % NX
        part = sall.at[k, group, pl.ds(side * (RP // 2), RP // 2)]
        return remote(part, part, x_send, xr_recv, xpeers[side])

    def signs(bits):
        return (1 - 2 * bits).astype(jnp.float32).astype(jnp.bfloat16)

    pl.semaphore_wait(barrier, len(peers))
    for half in range(NE):
        for sign in range(2):
            ring(sign, half, 0).start()
    loads[0].wait()
    pair(0, 0).start()
    for k in range(1, NY):
        sign_rows(k).wait()
        sout[k - 1] = signs(sfor[k - 1])
        s_copy(k).start()
    loads[1].wait()
    rows_blk = h_ref.shape[0]
    hbuf[0:rows_blk] = hin[...].astype(jnp.float32)
    hbuf[rows_blk:RP] = jnp.zeros((RP - rows_blk, NE, TOK), jnp.float32)
    lane = lax.broadcasted_iota(jnp.int32, (RP, TOK), 1)
    for e in range(NE):
        mall[0, e] = jnp.where(lane < len_ref[e], hbuf[:, e, :], 0.0).astype(jnp.bfloat16)
    for side in range(2):
        m_copy(side, side).start()
    for side in range(2):
        m_copy(side, 1 - side).start()
    loads[2].wait()
    loads[3].wait()
    kpos = jnp.bitwise_and(kr_ref[...], 127)
    idx_ref[...] = (kpos >> 3) * (NG * GW) + jnp.bitwise_and(kc_ref[...], NG * GW - 1)
    to_smem = pltpu.make_async_copy(idx_ref, idx_smem, idx_sem)
    to_smem.start()
    sign_rows(0).wait()
    for g in range(NG):
        sall[0, g] = signs(sown[:, GW * g:GW * g + GW])
    h256 = sylvester_tile(GW, GW, 255, 255).astype(jnp.bfloat16)

    def step(s):
        for half in range(NE):
            for sign in range(2):
                ring(sign, half, s, True).wait_recv()
                if s < 7 or half // 2 == sign:
                    ring(sign, half, s).start()
        if s == 7:
            for sign in range(2):
                last_ring(sign).start()
        for sign in range(2):
            pair(sign, s).start()

    def compute(g):
        turned = [sall[b, g].astype(jnp.float32) for b in range(NY)]
        for e in range(NE):
            lhs = mall[:, e].reshape(NY * RP, TOK)
            rhs = cols[pl.ds(NG * g, NG), :, e].reshape(GW, TOK)
            grad = lax.dot_general(lhs, rhs, NT, preferred_element_type=jnp.float32)
            for b in range(NY):
                w = grad[RP * b:RP * b + RP] * turned[b]
                for k in range(NK):
                    wbuf[k, 32 * b + 8 * e:32 * b + 8 * e + 8] = w[8 * k:8 * k + 8]
        for k in range(0, NK, 2):
            n = min(2, NK - k)
            hi, lo = split(wbuf[k:k + n].reshape(128 * n, GW))
            out = (lax.dot_general(h256, hi, NT, preferred_element_type=jnp.float32)
                   + lax.dot_general(h256, lo, NT, preferred_element_type=jnp.float32))
            for i in range(n):
                xs[k + i] = out[:, 128 * i:128 * i + 128]

    step(1)
    step(2)
    for k in (1, 3, 2):
        s_copy(k, True).wait_recv()
        for side in range(2):
            x_copy(side, NY - k).start()
    step(3)
    pick, finish = make_picker(kr_ref, kc_ref, idx_smem, table, pbuf, hot, wpick, y, z * NC + c, scale)
    step(4)
    for side in range(2):
        m_copy(side, side, True).wait_recv()
        m_relay(side).start()
    for k in (3, 1, 2):
        for side in range(2):
            x_copy(side, k, True).wait_recv()
            x_relay(side, k).start()
    flat = table
    mine = z // NG
    low = z % NG < 2
    early = jnp.where(low, (mine + NG - 1) % NG, (mine + 1) % NG)
    late = jnp.where(low, (mine + 1) % NG, (mine + NG - 1) % NG)

    def stage(t, carry):
        @pl.when(t == 0)
        def _():
            step(5)
            step(6)
            landed(cols.at[pl.ds(0, 7), 0], p_recv.at[0])
            for side in range(2):
                m_copy(side, 1 - side, True).wait_recv()
                m_relay(side, True).wait_recv()
            landed(sall.at[pl.ds(1, NY - 1), 0], xr_recv)

        @pl.when(t == 1)
        def _():
            step(7)
            landed(cols.at[pl.ds(0, 4), 0], p_recv.at[1])

        @pl.when(t == 2)
        def _():
            landed(cols.at[pl.ds(0, 4), 0], p_recv.at[2])

        @pl.when(t == 3)
        def _():
            for sign in range(2):
                for half in (2 * sign, 2 * sign + 1):
                    ring(sign, half, 8, True).wait_recv()
            landed(cols.at[0, 0], c_recv)

        g = jnp.where(t == 0, mine, jnp.where(t == 1, early, jnp.where(t == 2, late, (mine + 2) % NG)))
        compute(g)
        spread_rows(xs, flat, g)
        return carry

    lax.fori_loop(0, NG, stage, 0)
    join_groups(flat)
    to_smem.wait()
    quarter = pbuf.shape[0] // NY
    per = quarter // LINES

    def y_copy(k):
        far = (y + k) % NY
        return remote(pbuf.at[pl.ds(far * quarter, quarter)], ybuf.at[k - 1], ysend, yrecv,
                      device(far, z, c, x))

    def turn(q):
        return jnp.where(q == 0, 2, jnp.where(q == 1, 1, 3))

    def chunk_at(j):
        other = ((y + turn(j // per)) % NY) * per + j % per
        off = jnp.where(j == 12, 2, jnp.where(j == 13, 1, jnp.where(j == 14, 3, 0)))
        return jnp.where(j < 12, other, y * per + (z // LINES + off) % per)

    def z_copy(k):
        far = (z + k) % NZ
        return remote(zsum.at[far], zbuf.at[k - 1], zsend, zrecv, device(y, far, c, x))

    def add_up(far):
        total = pbuf[y * quarter + far]
        for k in range(1, NY):
            total = total + ybuf[k - 1, far]
        zsum[far] = total

    def emit(j, own):
        first = LINES * (chunk_at(j) - y * per)
        for h in range(LINES):
            far = first + h
            add_up(far)
            if own:
                @pl.when(far != z)
                def _():
                    z_copy((far + NZ - z) % NZ).start()
            else:
                z_copy((far + NZ - z) % NZ).start()

    def drain():
        landed(cols.at[pl.ds(0, NZ - 1)], r_send)
        landed(cols.at[0, 0], c_send)
        landed(mall.at[pl.ds(0, NY - 1)], m_send)
        landed(sout, s_send)
        landed(sall.at[pl.ds(0, 3), pl.ds(0, 3)], x_send)

    pick(chunk_at(0), rows_a)

    def body(n, carry):
        pick(chunk_at(2 * n + 1), rows_b)
        finish(chunk_at(2 * n), rows_a)
        pick(chunk_at(2 * n + 2), rows_a)
        finish(chunk_at(2 * n + 1), rows_b)

        @pl.when((n < 6) & (n % 2 == 1))
        def _():
            y_copy(turn(n // 2)).start()

        return carry

    lax.fori_loop(0, 7, body, 0)
    pick(chunk_at(15), rows_b)
    finish(chunk_at(14), rows_a)
    landed(ybuf, yrecv)
    for j in (12, 13, 14):
        emit(j, False)
    finish(chunk_at(15), rows_b)
    emit(15, True)
    drain()
    landed(zbuf, zrecv)
    total = zsum[z]
    for k in range(1, NZ):
        total = total + zbuf[k - 1]
    tbuf[...] = total

    def last_copy(i):
        return remote(tbuf, xbuf.at[i], xsend, xrecv, square[i])

    for i in range(len(offsets)):
        last_copy(i).start()
    landed(ybuf, ysend)
    landed(zbuf, zsend)
    landed(xbuf, xrecv)
    slot = {o: i for i, o in enumerate(offsets)}
    for dx in range(NX):
        first = total if dx == 0 else xbuf[slot[(0, dx)]]
        out_ref[(x - dx + NX) % NX] = first + xbuf[slot[(1, dx)]]

    landed(xbuf, xsend)


def local(hidden, out_grad, example_len, sign_bits, kept_rows, kept_cols):
    keep = kept_rows.shape[0]
    total_len = sign_bits.shape[0] * lax.axis_size("blk") * sign_bits.shape[1]
    blk_index = lax.axis_index("blk")
    dma = pltpu.SemaphoreType.DMA
    vm = pl.BlockSpec(memory_space=pltpu.VMEM)
    hbm = pl.BlockSpec(memory_space=pl.ANY)

    f32 = jnp.float32
    blocks = pl.pallas_call(
        functools.partial(sketch_kernel, scale=1.0 / math.sqrt(total_len)),
        out_shape=jax.ShapeDtypeStruct((NX, NE, 128), f32),
        in_specs=[hbm, hbm, pl.BlockSpec(memory_space=pltpu.SMEM), hbm, hbm, hbm],
        out_specs=vm,
        scratch_shapes=[
            pltpu.VMEM((NZ, NC, NE, JW, TOK), jnp.bfloat16),
            pltpu.VMEM((keep // 128, 128), jnp.int32), pltpu.VMEM((keep // 128, 128), jnp.int32),
            pltpu.VMEM((hidden.shape[2], NE, TOK), jnp.bfloat16),
            pltpu.VMEM((NY, NE, RP, TOK), jnp.bfloat16),
            pltpu.VMEM((NY, NG, RP, GW), jnp.bfloat16),
            pltpu.VMEM((NY - 1, RP, GW), jnp.bfloat16),
            pltpu.VMEM((RP, NE, TOK), f32),
            pltpu.VMEM((RP, NG * GW), jnp.int32),
            pltpu.VMEM((NY - 1, RP, GW), jnp.int32),
            pltpu.VMEM((NK, 128, GW), f32),
            pltpu.VMEM((NK, GW, 128), f32),
            pltpu.VMEM((KHI * NG * GW, 128), f32),
            pltpu.VMEM((CH, 128), f32), pltpu.VMEM((CH, 128), f32),
            pltpu.VMEM((keep // 128, 32, 128), f32), pltpu.VMEM((128, 256), jnp.bfloat16),
            pltpu.VMEM((keep // 128, 128), jnp.int32), pltpu.SMEM((keep // 128, 128), jnp.int32),
            pltpu.VMEM((keep // 128, NE, 128), f32),
            pltpu.VMEM((NY - 1, NZ, NE, 128), f32),
            pltpu.VMEM((NZ, NE, 128), f32),
            pltpu.VMEM((NZ - 1, NE, 128), f32),
            pltpu.VMEM((NE, 128), f32),
            pltpu.VMEM((7, NE, 128), f32),
            dma, dma((2, NE, 9)), dma((3,)), dma, dma((3, 2)),
            dma, dma((NY - 1,)), dma, dma((2, NY - 1)), dma,
            dma, dma, dma((4,)), dma, dma((NY,)), dma, dma, dma, dma, dma, dma,
        ],
        compiler_params=pltpu.CompilerParams(
            collective_id=0, has_side_effects=True, vmem_limit_bytes=VMEM_MB),
    )(out_grad.transpose(0, 2, 1), hidden.transpose(2, 0, 1), example_len, sign_bits,
      kept_rows.reshape(keep // 128, 128), kept_cols.reshape(keep // 128, 128))
    start = (blk_index % NC) * 64 + lax.axis_index("ex") * 16
    return lax.dynamic_slice_in_dim(blocks.reshape(4 * NE, 128), start, 16, axis=1)


def solution(mesh):
    return jax.shard_map(
        local,
        mesh=mesh,
        in_specs=(P("ex", None, "blk"), P("ex", None, "blk"), P("ex"), P("blk", None), P(), P()),
        out_specs=P(None, ("blk", "ex")),
        check_vma=False,
    )
```

```python
import functools
import math

import jax
import jax.numpy as jnp
from jax import lax
from jax.experimental import pallas as pl
from jax.experimental.pallas import tpu as pltpu
from jax.sharding import PartitionSpec as P

NY, NZ, NC, NX = 4, 16, 2, 4
NE = 4
TOK = 256
JW = 32
RP = 96
NK = 11
NG = 4
GW = 256
VMEM_MB = 56 << 20
NT = (((1,), (1,)), ((), ()))
TN = (((0,), (0,)), ((), ()))


def parity(bits):
    for shift_by in (16, 8, 4, 2, 1):
        bits = jnp.bitwise_xor(bits, jnp.right_shift(bits, shift_by))
    return jnp.bitwise_and(bits, 1)


def sylvester_tile(rows, cols, row_mask, col_mask):
    a = jnp.bitwise_and(lax.broadcasted_iota(jnp.int32, (rows, cols), 0), row_mask)
    b = jnp.bitwise_and(lax.broadcasted_iota(jnp.int32, (rows, cols), 1), col_mask)
    return (1 - 2 * parity(jnp.bitwise_and(a, b))).astype(jnp.float32)


def split(values):
    hi = values.astype(jnp.bfloat16)
    lo = (values - hi.astype(jnp.float32)).astype(jnp.bfloat16)
    return hi, lo


def device(y, z, c, x):
    return ((y * NZ + z) * NC + c, x)


def place():
    b = lax.axis_index("blk")
    return b // (NZ * NC), (b // NC) % NZ, b % NC, lax.axis_index("ex")


def butterfly(values, width):
    values = list(values) + [None] * (width - len(values))
    step = width // 2
    while step:
        for base in range(0, width, 2 * step):
            for j in range(base, base + step):
                a, b = values[j], values[j + step]
                values[j], values[j + step] = (a, a) if b is None else (a + b, a - b)
        step //= 2
    return values


LINES = 4
CH = LINES * 128
GROUP = 32
KHI = 16


def spread_rows(xs, flat, g):
    def mix(rb, carry):
        rows = pl.ds(pl.multiple_of(rb * 8, 8), 8)
        for p, v in enumerate(butterfly([xs[k, rows, :] for k in range(NK)], KHI)):
            flat[pl.ds(pl.multiple_of((p * NG + g) * GW + rb * 8, 8), 8), :] = v
        return carry

    lax.fori_loop(0, GW // 8, mix, 0, unroll=4)


def join_groups(flat):
    def mix(rb, carry):
        for p in range(KHI):
            rows = [pl.ds(pl.multiple_of((p * NG + g) * GW + rb * 8, 8), 8) for g in range(NG)]
            for g, v in enumerate(butterfly([flat[r, :] for r in rows], NG)):
                flat[rows[g], :] = v
        return carry

    lax.fori_loop(0, GW // 8, mix, 0, unroll=2)


def make_picker(kr_ref, kc_ref, idx_smem, table_ref, out_ref, hot, wpick, y, zc, scale):
    row = lax.broadcasted_iota(jnp.int32, (128, 128), 0)
    lane = lax.broadcasted_iota(jnp.int32, (128, 128), 1)
    owner = jnp.bitwise_and((lane >> 5) + y, NY - 1)
    code = row & 31
    bits = jnp.bitwise_or(jnp.bitwise_and(code >> 3, owner) << 3, jnp.bitwise_and(code, lane) & 7)
    hx = (1 - 2 * parity(bits)).astype(jnp.float32)
    hx = jnp.where((row >> 5) == ((lane >> 3) & (NE - 1)), hx, 0.0).astype(jnp.bfloat16)
    wpick[...] = jnp.concatenate([hx, hx], axis=1)
    which = lax.broadcasted_iota(jnp.int32, (32, 128), 0)

    def prepare(line, carry):
        kr = kr_ref[pl.ds(line, 1), :]
        kc = kc_ref[pl.ds(line, 1), :]
        flips = jnp.bitwise_xor(jnp.bitwise_and((kr >> 7) & 31, zc), jnp.bitwise_and(kc >> 10, y) << 5)
        sign = (1 - 2 * parity(flips)).astype(jnp.float32) * scale
        hot[line] = jnp.where(which == ((kr >> 12) << 3) + jnp.bitwise_and(kr, 7), sign, 0.0)
        return carry

    lax.fori_loop(0, kr_ref.shape[0], prepare, 0, unroll=4)

    def pick(ch, rows_ref):
        for h in range(LINES):
            line = ch * LINES + h
            for g in range(128 // GROUP):
                rows = [table_ref[pl.ds(idx_smem[line, g * GROUP + u], 1), :] for u in range(GROUP)]
                for u in range(GROUP):
                    rows_ref[pl.ds(h * 128 + g * GROUP + u, 1), :] = rows[u]

    def finish(ch, rows_ref):
        onehot = jnp.concatenate([hot[ch * LINES + h] for h in range(LINES)], axis=1)
        hi, lo = split(rows_ref[...])
        both = jnp.concatenate([hi, lo], axis=1)
        prod = lax.dot_general(wpick[...], both, NT, preferred_element_type=jnp.float32)
        for e in range(NE):
            res = jnp.sum(prod[32 * e:32 * e + 32] * onehot, axis=0, keepdims=True)
            for h in range(LINES):
                out_ref[ch * LINES + h, pl.ds(e, 1), :] = res[:, 128 * h:128 * h + 128]

    return pick, finish


def remote(src, dst, send, recv, target):
    return pltpu.make_async_remote_copy(
        src_ref=src, dst_ref=dst, send_sem=send, recv_sem=recv,
        device_id=target, device_id_type=pl.DeviceIdType.MESH)


def landed(ref, sem):
    pltpu.make_async_copy(ref, ref, sem).wait()


def greet(peers):
    barrier = pltpu.get_barrier_semaphore()
    for peer in peers:
        pl.semaphore_signal(barrier, inc=1, device_id=peer, device_id_type=pl.DeviceIdType.MESH)
    return barrier


def sketch_kernel(own_ref, h_ref, len_ref, sb_ref, krh_ref, kch_ref, out_ref,
                  cols, kr_ref, kc_ref, hin, mall, sall, sout, hbuf, sown, sfor, wbuf, xs, table, rows_a, rows_b, hot, wpick, idx_ref, idx_smem,
                  pbuf, ybuf, zsum, zbuf, tbuf, xbuf, res,
                  r_send, r_recv, p_recv, m_send, m_recv, s_send, s_recv, x_send, x_recv, xr_recv,
                  c_send, c_recv, load_sem, idx_sem, sb_sem, ysend, yrecv, zsend, zrecv, xsend, xrecv, *, scale):
    y, z, c, x = place()
    zpeers = (device(y, (z + 1) % NZ, c, x), device(y, (z + NZ - 1) % NZ, c, x))
    sibling = device(y, z, 1 - c, x)
    ypeers = [device((y + k) % NY, z, c, x) for k in range(1, NY)]
    xpeers = (device(y, z, c, (x + 1) % NX), device(y, z, c, (x + NX - 1) % NX))
    zall = [device(y, (z + k) % NZ, c, x) for k in range(1, NZ)]
    offsets = [(dc, dx) for dx in range(NX) for dc in range(NC) if dc or dx]
    square = [device(y, z, (c + dc) % NC, (x + dx) % NX) for dc, dx in offsets]
    cross = (device(y, (z + 1) % NZ, 1 - c, x), device(y, (z + NZ - 1) % NZ, 1 - c, x))
    peers = list(zpeers) + list(cross) + ypeers + square + zall[1:-1]
    barrier = greet(peers)

    def sign_rows(k):
        width = GW if k else NG * GW
        start = ((y + k) % NY) * (NG * GW) + (x * GW if k else 0)
        src = sb_ref.at[pl.ds(0, RP), pl.ds(pl.multiple_of(start, GW), width)]
        return pltpu.make_async_copy(src, sfor.at[k - 1] if k else sown, sb_sem.at[k])

    loads = [pltpu.make_async_copy(src, dst, load_sem.at[i]) for i, (src, dst) in enumerate((
        (own_ref, cols.at[z, c]), (h_ref, hin), (krh_ref, kr_ref), (kch_ref, kc_ref)))]

    def slab(sign, s):
        return (z + NZ - s) % NZ if sign == 0 else (z + s) % NZ

    def ring(sign, half, s, arrival=False):
        part = cols.at[slab(sign, s), c, half]
        first = isinstance(s, int) and s == 0 and not arrival
        return remote(own_ref.at[half] if first else part, part, r_send,
                      r_recv.at[sign, half, s if arrival else s + 1], zpeers[sign])

    def last_ring(sign, arrival=False):
        part = cols.at[slab(sign, 8 if arrival else 7), 1 - c if arrival else c, pl.ds(2 * sign, 2)]
        return remote(part, part, c_send, c_recv, cross[sign])

    def pair(sign, s, arrival=False):
        part = cols.at[slab(sign, s), 1 - c if arrival else c]
        return remote(part, part, r_send, p_recv.at[0 if s < 4 else (1 if s < 6 else 2)], sibling)

    def m_copy(side, part, arrival=False):
        there = 3 if side == 0 else 1
        piece = pl.ds(2 * part, 2)
        dst = mall.at[there, piece]
        return remote(dst if arrival else mall.at[0, piece], dst, m_send, m_recv.at[side, 0 if part == side else 1],
                      ypeers[0] if side == 0 else ypeers[2])

    def m_relay(side, arrival=False):
        part = pl.ds(2 * side, 2)
        dst = mall.at[2, part]
        src = mall.at[3 if side == 0 else 1, part]
        return remote(dst if arrival else src, dst, m_send, m_recv.at[2, side],
                      ypeers[0] if side == 0 else ypeers[2])

    def s_copy(k, arrival=False):
        dst = sall.at[NY - k, x]
        return remote(dst if arrival else sout.at[k - 1], dst, s_send, s_recv.at[k - 1], ypeers[k - 1])

    def x_copy(side, k, arrival=False):
        group = x if not arrival else ((x + NX - 1) % NX if side == 0 else (x + 1) % NX)
        part = sall.at[k, group]
        return remote(part, part, x_send, x_recv.at[side, k - 1], xpeers[side])

    def x_relay(side, k):
        group = (x + NX - 1) % NX if side == 0 else (x + 1) % NX
        part = sall.at[k, group, pl.ds(side * (RP // 2), RP // 2)]
        return remote(part, part, x_send, xr_recv, xpeers[side])

    def signs(bits):
        return (1 - 2 * bits).astype(jnp.float32).astype(jnp.bfloat16)

    pl.semaphore_wait(barrier, len(peers))
    for half in range(NE):
        for sign in range(2):
            ring(sign, half, 0).start()
    loads[0].start()
    for k in (1, 2, 3):
        sign_rows(k).start()
    for load in loads[1:]:
        load.start()
    sign_rows(0).start()
    loads[0].wait()
    pair(0, 0).start()
    for k in range(1, NY):
        sign_rows(k).wait()
        sout[k - 1] = signs(sfor[k - 1])
        s_copy(k).start()
    loads[1].wait()
    rows_blk = h_ref.shape[0]
    hbuf[0:rows_blk] = hin[...].astype(jnp.float32)
    hbuf[rows_blk:RP] = jnp.zeros((RP - rows_blk, NE, TOK), jnp.float32)
    lane = lax.broadcasted_iota(jnp.int32, (RP, TOK), 1)
    for e in range(NE):
        mall[0, e] = jnp.where(lane < len_ref[e], hbuf[:, e, :], 0.0).astype(jnp.bfloat16)
    for side in range(2):
        m_copy(side, side).start()
    for side in range(2):
        m_copy(side, 1 - side).start()
    loads[2].wait()
    loads[3].wait()
    kpos = jnp.bitwise_and(kr_ref[...], 127)
    idx_ref[...] = (kpos >> 3) * (NG * GW) + jnp.bitwise_and(kc_ref[...], NG * GW - 1)
    to_smem = pltpu.make_async_copy(idx_ref, idx_smem, idx_sem)
    to_smem.start()
    sign_rows(0).wait()
    for g in range(NG):
        sall[0, g] = signs(sown[:, GW * g:GW * g + GW])
    h256 = sylvester_tile(GW, GW, 255, 255).astype(jnp.bfloat16)

    def step(s):
        for half in range(NE):
            for sign in range(2):
                ring(sign, half, s, True).wait_recv()
                if s < 7 or half // 2 == sign:
                    ring(sign, half, s).start()
        if s == 7:
            for sign in range(2):
                last_ring(sign).start()
        for sign in range(2):
            pair(sign, s).start()

    def compute(g):
        turned = [sall[b, g].astype(jnp.float32) for b in range(NY)]
        for e in range(NE):
            lhs = mall[:, e].reshape(NY * RP, TOK)
            rhs = cols[pl.ds(NG * g, NG), :, e].reshape(GW, TOK)
            grad = lax.dot_general(lhs, rhs, NT, preferred_element_type=jnp.float32)
            for b in range(NY):
                w = grad[RP * b:RP * b + RP] * turned[b]
                for k in range(NK):
                    wbuf[k, 32 * b + 8 * e:32 * b + 8 * e + 8] = w[8 * k:8 * k + 8]
        for k in range(0, NK, 2):
            n = min(2, NK - k)
            hi, lo = split(wbuf[k:k + n].reshape(128 * n, GW))
            out = (lax.dot_general(h256, hi, NT, preferred_element_type=jnp.float32)
                   + lax.dot_general(h256, lo, NT, preferred_element_type=jnp.float32))
            for i in range(n):
                xs[k + i] = out[:, 128 * i:128 * i + 128]

    step(1)
    step(2)
    for k in (1, 3, 2):
        s_copy(k, True).wait_recv()
        for side in range(2):
            x_copy(side, NY - k).start()
    step(3)
    pick, finish = make_picker(kr_ref, kc_ref, idx_smem, table, pbuf, hot, wpick, y, z * NC + c, scale)
    step(4)
    for side in range(2):
        m_copy(side, side, True).wait_recv()
        m_relay(side).start()
    for k in (3, 1, 2):
        for side in range(2):
            x_copy(side, k, True).wait_recv()
            x_relay(side, k).start()
    flat = table
    mine = z // NG
    low = z % NG < 2
    early = jnp.where(low, (mine + NG - 1) % NG, (mine + 1) % NG)
    late = jnp.where(low, (mine + 1) % NG, (mine + NG - 1) % NG)

    def stage(t, carry):
        @pl.when(t == 0)
        def _():
            step(5)
            step(6)
            landed(cols.at[pl.ds(0, 7), 0], p_recv.at[0])
            for side in range(2):
                m_copy(side, 1 - side, True).wait_recv()
                m_relay(side, True).wait_recv()
            landed(sall.at[pl.ds(1, NY - 1), 0], xr_recv)

        @pl.when(t == 1)
        def _():
            step(7)
            landed(cols.at[pl.ds(0, 4), 0], p_recv.at[1])

        @pl.when(t == 2)
        def _():
            landed(cols.at[pl.ds(0, 4), 0], p_recv.at[2])

        @pl.when(t == 3)
        def _():
            for sign in range(2):
                for half in (2 * sign, 2 * sign + 1):
                    ring(sign, half, 8, True).wait_recv()
            landed(cols.at[0, 0], c_recv)

        g = jnp.where(t == 0, mine, jnp.where(t == 1, early, jnp.where(t == 2, late, (mine + 2) % NG)))
        compute(g)
        spread_rows(xs, flat, g)
        return carry

    lax.fori_loop(0, NG, stage, 0)
    join_groups(flat)
    to_smem.wait()
    quarter = pbuf.shape[0] // NY
    per = quarter // LINES

    def y_copy(k):
        far = (y + k) % NY
        return remote(pbuf.at[pl.ds(far * quarter, quarter)], ybuf.at[k - 1], ysend, yrecv,
                      device(far, z, c, x))

    def turn(q):
        return jnp.where(q == 0, 2, jnp.where(q == 1, 1, 3))

    def chunk_at(j):
        other = ((y + turn(j // per)) % NY) * per + j % per
        off = jnp.where(j == 12, 2, jnp.where(j == 13, 1, jnp.where(j == 14, 3, 0)))
        return jnp.where(j < 12, other, y * per + (z // LINES + off) % per)

    def z_copy(k):
        far = (z + k) % NZ
        return remote(zsum.at[far], zbuf.at[k - 1], zsend, zrecv, device(y, far, c, x))

    def add_up(far):
        total = pbuf[y * quarter + far]
        for k in range(1, NY):
            total = total + ybuf[k - 1, far]
        zsum[far] = total

    def emit(j, own):
        first = LINES * (chunk_at(j) - y * per)
        for h in range(LINES):
            far = first + h
            add_up(far)
            if own:
                @pl.when(far != z)
                def _():
                    z_copy((far + NZ - z) % NZ).start()
            else:
                z_copy((far + NZ - z) % NZ).start()

    def drain():
        landed(cols.at[pl.ds(0, NZ - 1)], r_send)
        landed(cols.at[0, 0], c_send)
        landed(mall.at[pl.ds(0, NY - 1)], m_send)
        landed(sout, s_send)
        landed(sall.at[pl.ds(0, 3), pl.ds(0, 3)], x_send)

    pick(chunk_at(0), rows_a)

    def body(n, carry):
        pick(chunk_at(2 * n + 1), rows_b)
        finish(chunk_at(2 * n), rows_a)
        pick(chunk_at(2 * n + 2), rows_a)
        finish(chunk_at(2 * n + 1), rows_b)

        @pl.when((n < 6) & (n % 2 == 1))
        def _():
            y_copy(turn(n // 2)).start()

        return carry

    lax.fori_loop(0, 7, body, 0)
    pick(chunk_at(15), rows_b)
    finish(chunk_at(14), rows_a)
    landed(ybuf, yrecv)
    for j in (12, 13, 14):
        emit(j, False)
    finish(chunk_at(15), rows_b)
    emit(15, True)
    drain()
    landed(zbuf, zrecv)
    total = zsum[z]
    for k in range(1, NZ):
        total = total + zbuf[k - 1]
    tbuf[...] = total

    def last_copy(i):
        return remote(tbuf, xbuf.at[i], xsend, xrecv, square[i])

    for i in range(len(offsets)):
        last_copy(i).start()
    landed(ybuf, ysend)
    landed(zbuf, zsend)
    landed(xbuf, xrecv)
    slot = {o: i for i, o in enumerate(offsets)}
    for dx in range(NX):
        first = total if dx == 0 else xbuf[slot[(0, dx)]]
        res[(x - dx + NX) % NX] = first + xbuf[slot[(1, dx)]]
    rows = res[...].reshape(NX * NE, 128)
    mine_now = c * NX + x
    owned = rows[:, 0:16]
    for i in range(1, NC * NX):
        owned = jnp.where(mine_now == i, rows[:, 16 * i:16 * i + 16], owned)
    out_ref[...] = owned

    landed(xbuf, xsend)


def local(hidden, out_grad, example_len, sign_bits, kept_rows, kept_cols):
    keep = kept_rows.shape[0]
    total_len = sign_bits.shape[0] * lax.axis_size("blk") * sign_bits.shape[1]
    dma = pltpu.SemaphoreType.DMA
    vm = pl.BlockSpec(memory_space=pltpu.VMEM)
    hbm = pl.BlockSpec(memory_space=pl.ANY)

    f32 = jnp.float32
    return pl.pallas_call(
        functools.partial(sketch_kernel, scale=1.0 / math.sqrt(total_len)),
        out_shape=jax.ShapeDtypeStruct((NX * NE, 16), f32),
        in_specs=[hbm, hbm, pl.BlockSpec(memory_space=pltpu.SMEM), hbm, hbm, hbm],
        out_specs=vm,
        scratch_shapes=[
            pltpu.VMEM((NZ, NC, NE, JW, TOK), jnp.bfloat16),
            pltpu.VMEM((keep // 128, 128), jnp.int32), pltpu.VMEM((keep // 128, 128), jnp.int32),
            pltpu.VMEM((hidden.shape[2], NE, TOK), jnp.bfloat16),
            pltpu.VMEM((NY, NE, RP, TOK), jnp.bfloat16),
            pltpu.VMEM((NY, NG, RP, GW), jnp.bfloat16),
            pltpu.VMEM((NY - 1, RP, GW), jnp.bfloat16),
            pltpu.VMEM((RP, NE, TOK), f32),
            pltpu.VMEM((RP, NG * GW), jnp.int32),
            pltpu.VMEM((NY - 1, RP, GW), jnp.int32),
            pltpu.VMEM((NK, 128, GW), f32),
            pltpu.VMEM((NK, GW, 128), f32),
            pltpu.VMEM((KHI * NG * GW, 128), f32),
            pltpu.VMEM((CH, 128), f32), pltpu.VMEM((CH, 128), f32),
            pltpu.VMEM((keep // 128, 32, 128), f32), pltpu.VMEM((128, 256), jnp.bfloat16),
            pltpu.VMEM((keep // 128, 128), jnp.int32), pltpu.SMEM((keep // 128, 128), jnp.int32),
            pltpu.VMEM((keep // 128, NE, 128), f32),
            pltpu.VMEM((NY - 1, NZ, NE, 128), f32),
            pltpu.VMEM((NZ, NE, 128), f32),
            pltpu.VMEM((NZ - 1, NE, 128), f32),
            pltpu.VMEM((NE, 128), f32),
            pltpu.VMEM((7, NE, 128), f32),
            pltpu.VMEM((NX, NE, 128), f32),
            dma, dma((2, NE, 9)), dma((3,)), dma, dma((3, 2)),
            dma, dma((NY - 1,)), dma, dma((2, NY - 1)), dma,
            dma, dma, dma((4,)), dma, dma((NY,)), dma, dma, dma, dma, dma, dma,
        ],
        compiler_params=pltpu.CompilerParams(
            collective_id=0, has_side_effects=True, vmem_limit_bytes=VMEM_MB),
    )(out_grad.transpose(0, 2, 1), hidden.transpose(2, 0, 1), example_len, sign_bits,
      kept_rows.reshape(keep // 128, 128), kept_cols.reshape(keep // 128, 128))


def solution(mesh):
    return jax.shard_map(
        local,
        mesh=mesh,
        in_specs=(P("ex", None, "blk"), P("ex", None, "blk"), P("ex"), P("blk", None), P(), P()),
        out_specs=P(None, ("blk", "ex")),
        check_vma=False,
    )
```
